256 devices in a mesh: dp: 32 (over z_lo, x, core), tensor: 8 (over y, z_hi).
Axes of the slice: x: 4, y: 4, z: 8 (z_hi: 2, z_lo: 4; z = z_hi * 4 + z_lo), core: 2. Of those that a mesh axis runs over, the one named last changes fastest.
Arguments:
- inputs: bfloat16 [768, 8192], P('dp', 'tensor'), may hold values from -6 to 6
- grad_out: bfloat16 [768, 8192], P('dp', 'tensor'), may hold values from -6 to 6
- w_gate: bfloat16 [8192, 28672], P('tensor', 'dp'), may hold values from -0.0625 to 0.0625
- w_up: bfloat16 [8192, 28672], P('tensor', 'dp'), may hold values from -0.0625 to 0.0625
- w_down: bfloat16 [28672, 8192], P('dp', 'tensor'), may hold values from -0.03125 to 0.03125
Outputs:
- grad_in: bfloat16 [768, 8192], P('dp', 'tensor')
- grad_gate: bfloat16 [8192, 28672], P('tensor', 'dp')
- grad_up: bfloat16 [8192, 28672], P('tensor', 'dp')
- grad_down: bfloat16 [28672, 8192], P('dp', 'tensor')
The draws below stay inside these ranges and needn't reach their ends.
All inputs are finite; a program needn't handle non-finite values.
Results may differ from the reference program's by a relative error of at most 0.0049.
Values may be sent and summed in bfloat16 or wider, within the bound.
No kernel may reach another device: no remote copies, remote signals or barrier semaphores. Data moves between devices by JAX's collectives and lax.ppermute only.
A program may use at most 128 MiB of HBM per device.

```python
import jax
import jax.numpy as jnp

D = 8192
FF = 28672
TOKENS = 768


def block_scale(stream_key, dims, split, low, largest):
    def one(axis_at, blocks):
        draws = jax.random.uniform(jax.random.fold_in(jax.random.fold_in(stream_key, 6), axis_at), (blocks,), jnp.float32, low / len(split), largest / len(split))
        return jnp.repeat(jnp.exp(draws), dims[axis_at] // blocks).reshape((-1,) + (1,) * (len(dims) - axis_at - 1))

    loudness = one(*split[0])
    for cut in split[1:]:
        loudness = loudness * one(*cut)
    return loudness


def noise(own_key, extent, width, reach, cuts=(), dtype=jnp.bfloat16):
    factor_of = block_scale(own_key, extent, cuts, -0.22, 0.18) if cuts else 1.0
    values = jax.random.normal(own_key, extent, jnp.float32) * width * factor_of
    return jnp.minimum(jnp.maximum(values, -reach), reach).astype(dtype)


def setup_inputs(seed: int = 0) -> dict:
    key_of = jax.random.split(jax.random.key(seed), 6)
    inputs = noise(key_of[0], (TOKENS, D), 1.0, 6.0, ((0, 32), (1, 8)))
    grad_out = noise(key_of[1], (TOKENS, D), 1.0, 6.0, ((0, 32), (1, 8)))
    w_gate = noise(key_of[2], (D, FF), D ** -0.5, 0.0625, ((0, 8), (1, 32)))
    w_up = noise(key_of[3], (D, FF), D ** -0.5, 0.0625, ((0, 8), (1, 32)))
    w_down = noise(key_of[4], (FF, D), FF ** -0.5, 0.03125, ((0, 32), (1, 8)))
    return dict(inputs=inputs, grad_out=grad_out, w_gate=w_gate, w_up=w_up, w_down=w_down)


def reference(inputs, grad_out, w_gate, w_up, w_down):
    gate_pre = jnp.dot(inputs, w_gate, preferred_element_type=jnp.float32)
    up_pre = jnp.dot(inputs, w_up, preferred_element_type=jnp.float32)
    hid_grad = jnp.dot(grad_out, w_down.T, preferred_element_type=jnp.float32)
    sig_gate = jax.nn.sigmoid(gate_pre)
    silu_gate = gate_pre * sig_gate
    hidden = (silu_gate * up_pre).astype(jnp.bfloat16)
    gate_grad = (hid_grad * up_pre * sig_gate * (1.0 + gate_pre * (1.0 - sig_gate))).astype(jnp.bfloat16)
    up_grad = (hid_grad * silu_gate).astype(jnp.bfloat16)
    grad_gate = jnp.dot(inputs.T, gate_grad, preferred_element_type=jnp.float32).astype(jnp.bfloat16)
    grad_up = jnp.dot(inputs.T, up_grad, preferred_element_type=jnp.float32).astype(jnp.bfloat16)
    grad_down = jnp.dot(hidden.T, grad_out, preferred_element_type=jnp.float32).astype(jnp.bfloat16)
    grad_in = jnp.dot(gate_grad, w_gate.T, preferred_element_type=jnp.float32)
    grad_in = grad_in + jnp.dot(up_grad, w_up.T, preferred_element_type=jnp.float32)
    return grad_in.astype(jnp.bfloat16), grad_gate, grad_up, grad_down
```

```python
import functools

import jax
import jax.numpy as jnp
from jax import lax
from jax.experimental import pallas as pl
from jax.experimental.pallas import tpu as pltpu
from jax.sharding import PartitionSpec as P

AXES = ("dp", "tensor")
F32 = jnp.float32
BF16 = jnp.bfloat16
ROWS = 48
WIDE = 1024
HID = 896
MIB = 1 << 20


def device_index(z, x, core, y):
    return (((z % 4) * 4 + x) * 2 + core) * 8 + y * 2 + z // 4


def swap(value, partner):
    pairs = [
        (device_index(z, x, c, y), device_index(*partner(z, x, c, y)))
        for z in range(8)
        for x in range(4)
        for c in range(2)
        for y in range(4)
    ]
    return lax.ppermute(value, AXES, pairs)


def swap_y(value, mask):
    return swap(value, lambda z, x, c, y: (z, x, c, y ^ mask))


def swap_z(value, mask):
    return swap(value, lambda z, x, c, y: (z ^ mask, x, c, y))


def swap_core(value):
    return swap(value, lambda z, x, c, y: (z, x, c ^ 1, y))


def swap_x(value, slot):
    return swap(value, lambda z, x, c, y: (z, x ^ y ^ slot, c, y))


def call(kernel, outs, args, flops, vmem):
    size = sum(a.size * a.dtype.itemsize for a in args)
    size += sum(o.size * o.dtype.itemsize for o in outs)
    whole = pl.BlockSpec(memory_space=pltpu.VMEM)
    return pl.pallas_call(
        kernel,
        out_shape=outs,
        in_specs=[whole] * len(args),
        out_specs=[whole] * len(outs),
        compiler_params=pltpu.CompilerParams(vmem_limit_bytes=vmem * MIB),
        cost_estimate=pl.CostEstimate(flops=flops, bytes_accessed=size, transcendentals=0),
    )(*args)


def shape(*dims, dtype=BF16):
    return jax.ShapeDtypeStruct(dims, dtype)


def forward_kernel(b0, b1, b2, b3, w_gate, w_up, w_down, far, near, own):
    blocks = (b0, b1, b2, b3)
    xs = jnp.concatenate([b[0] for b in blocks], axis=0)
    gs = jnp.concatenate([b[1] for b in blocks], axis=0)
    for i, (left, w, dim) in enumerate(((xs, w_gate, 0), (xs, w_up, 0), (gs, w_down, 1))):
        out = lax.dot_general(
            left, w[...], (((1,), (dim,)), ((), ())), preferred_element_type=F32
        )
        far[0, i] = out[:ROWS].astype(BF16)
        far[1, i] = out[ROWS : 2 * ROWS].astype(BF16)
        near[i] = out[2 * ROWS : 3 * ROWS]
        own[i] = out[3 * ROWS :]


def forward(blocks, weights, mask):
    order = (mask, 2, mask ^ 2, 0)
    return call(
        forward_kernel,
        [
            shape(2, 3, ROWS, HID),
            shape(3, ROWS, HID, dtype=F32),
            shape(3, ROWS, HID, dtype=F32),
        ],
        [blocks[k] for k in order] + list(weights),
        2 * 3 * 4 * ROWS * WIDE * HID,
        32,
    )


def grads_kernel(total, other, out):
    gate, up, hid = (total[i] + other[i].astype(F32) for i in range(3))
    sig = jax.nn.sigmoid(gate)
    silu = gate * sig
    out[0] = (silu * up).astype(BF16)
    out[1] = (hid * up * sig * (1.0 + gate * (1.0 - sig))).astype(BF16)
    out[2] = (hid * silu).astype(BF16)


def reduce_and_gather(blocks, weights, mask):
    last = mask ^ 2
    far, near, own = forward(blocks, weights, mask)
    far = swap_y(far, mask)
    near = swap_y((near + far[1].astype(F32)).astype(BF16), last)
    total = own + far[0].astype(F32) + near.astype(F32)
    other = swap_z(total.astype(BF16), 4)
    (grads,) = call(grads_kernel, [shape(3, ROWS, HID)], [total, other], 20 * 3 * ROWS * HID, 8)
    pair = jnp.stack([grads, swap_y(grads, last)])
    return pair, swap_y(pair, mask)


def backward_kernel(order, pair, rest, w_gate, w_up, out):
    total = 0.0
    for i, w in ((1, w_gate), (2, w_up)):
        left = jnp.concatenate([pair[0, i], pair[1, i], rest[0, i], rest[1, i]], axis=0)
        total += lax.dot_general(
            left, w[...], (((1,), (1,)), ((), ())), preferred_element_type=F32
        )
    for k, slot in enumerate(order):
        out[slot] = total[k * ROWS : (k + 1) * ROWS]


def backward(grads, w_gate, w_up, order):
    (out,) = call(
        functools.partial(backward_kernel, order),
        [shape(4, ROWS, WIDE, dtype=F32)],
        [*grads, w_gate, w_up],
        2 * 2 * 4 * ROWS * WIDE * HID,
        24,
    )
    return out


def join_kernel(mine, theirs, *outs):
    for k, out in enumerate(outs):
        out[...] = (mine[k] + theirs[k]).astype(BF16)


def reduce_x(own, other, w_gate, w_up):
    theirs = swap_core(backward(other, w_gate, w_up, (0, 1, 3, 2)))
    mine = backward(own, w_gate, w_up, (0, 3, 1, 2))
    parts = call(join_kernel, [shape(ROWS, WIDE)] * 4, [mine, theirs], 4 * ROWS * WIDE, 8)
    total = None
    for slot, part in enumerate(parts):
        term = swap_x(part, slot).astype(F32)
        total = term if total is None else total + term
    return total


def dot(left, right):
    return lax.dot_general(
        left, right, (((0,), (0,)), ((), ())), preferred_element_type=F32
    ).astype(BF16)


def body(inputs, grad_out, w_gate, w_up, w_down):
    weights = (w_gate, w_up, w_down)
    block = jnp.stack([inputs, grad_out])
    near = jnp.concatenate([block, swap_z(block, 1)], axis=1)
    far = swap_z(near, 2)
    groups, tokens, gathered = [], [], []
    for column in (near, far):
        own = [swap_x(column, k) for k in range(4)]
        other = [swap_core(b) for b in own]
        groups.append((reduce_and_gather(own, weights, 1), reduce_and_gather(other, weights, 3)))
        tokens += [own[k] for k in (0, 3, 1, 2)] + [other[k] for k in (0, 1, 3, 2)]
        for pair, rest in groups[-1]:
            gathered += [pair[0], pair[1], rest[0], rest[1]]

    sums = [reduce_x(own, other, w_gate, w_up) for own, other in groups]
    mine = sums[0] + swap_z(sums[1], 2)
    grad_in = (mine[:24] + swap_z(mine[24:], 1)).astype(BF16)

    rows_all, grads_all = (jnp.concatenate([b[i] for b in tokens], axis=0) for i in range(2))
    hidden, gate_grad, up_grad = (
        jnp.concatenate([b[i] for b in gathered], axis=0) for i in range(3)
    )
    return grad_in, dot(rows_all, gate_grad), dot(rows_all, up_grad), dot(hidden, grads_all)


def solution(mesh):
    return jax.shard_map(
        body,
        mesh=mesh,
        in_specs=(
            P("dp", "tensor"),
            P("dp", "tensor"),
            P("tensor", "dp"),
            P("tensor", "dp"),
            P("dp", "tensor"),
        ),
        out_specs=(P("dp", "tensor"), P("tensor", "dp"), P("tensor", "dp"), P("dp", "tensor")),
        check_vma=False,
    )
```

```python
import functools

import jax
import jax.numpy as jnp
from jax import lax
from jax.experimental import pallas as pl
from jax.experimental.pallas import tpu as pltpu
from jax.sharding import PartitionSpec as P

AXES = ("dp", "tensor")
F32 = jnp.float32
BF16 = jnp.bfloat16
PART = 24
ROWS = 4 * PART
WIDE = 1024
HID = 896
MIB = 1 << 20


def device_index(z, x, core, y):
    return (((z % 4) * 4 + x) * 2 + core) * 8 + y * 2 + z // 4


def swap(value, partner):
    pairs = [
        (device_index(z, x, c, y), device_index(*partner(z, x, c, y)))
        for z in range(8)
        for x in range(4)
        for c in range(2)
        for y in range(4)
    ]
    return lax.ppermute(value, AXES, pairs)


def swap_y(value, mask):
    return swap(value, lambda z, x, c, y: (z, x, c, y ^ mask))


def swap_z(value, mask):
    return swap(value, lambda z, x, c, y: (z ^ mask, x, c, y))


def swap_core(value):
    return swap(value, lambda z, x, c, y: (z, x, c ^ 1, y))


def swap_x(value, mask):
    return swap(value, lambda z, x, c, y: (z, x ^ mask, c, y))


VMEM = pl.BlockSpec(memory_space=pltpu.VMEM)
SMEM = pl.BlockSpec(memory_space=pltpu.SMEM)


def call(kernel, args, outs, vmem, later_than=(), y=None, scratch=(), flops=1):
    scalars = [] if y is None else [y]
    first, last = len(scalars), len(scalars) + len(args)

    def run(*refs):
        kernel(*refs[:last], *refs[last + len(later_than) :])

    return pl.pallas_call(
        run,
        out_shape=outs,
        in_specs=[SMEM] * first + [VMEM] * (len(args) + len(later_than)),
        out_specs=[VMEM] * len(outs),
        scratch_shapes=scratch,
        compiler_params=pltpu.CompilerParams(vmem_limit_bytes=vmem * MIB),
        cost_estimate=pl.CostEstimate(flops=flops, bytes_accessed=1, transcendentals=0),
    )(*scalars, *args, *later_than)


def shape(*dims, dtype=BF16):
    return jax.ShapeDtypeStruct(dims, dtype)


def touch_kernel(w_gate, w_up, out):
    out[...] = w_gate[:8, :128].astype(F32) + w_up[:8, :128].astype(F32)


def column_kernel(*refs):
    for i in range(4):
        refs[4][i * PART : (i + 1) * PART] = refs[i][...]


def products(tokens, weights, dims, sends, own):
    for i, (left, w, dim) in enumerate(zip(tokens, weights, dims)):
        out = lax.dot_general(
            left[...].reshape(4 * ROWS, WIDE),
            w[...],
            (((1,), (dim,)), ((), ())),
            preferred_element_type=F32,
        )
        for k, send in enumerate(sends):
            send[i] = out[(k + 1) * ROWS : (k + 2) * ROWS].astype(BF16)
        own[i] = out[:ROWS]


def gate_up_kernel(y_ref, *refs):
    blocks, weights, sends, own, xs = refs[:4], refs[4:6], refs[6:9], refs[9], refs[10]
    for j, block in enumerate(blocks):
        xs[j ^ y_ref[0]] = block[...]
    products((xs, xs), weights, (0, 0), sends, own)


def hid_kernel(y_ref, *refs):
    blocks, xs, w_down, sends, own, tokens = refs[:4], refs[4], refs[5], refs[6:9], refs[9], refs[10]
    tokens[0] = xs[...]
    for j, block in enumerate(blocks):
        tokens[1, j ^ y_ref[0]] = block[...]
    products((tokens.at[1],), (w_down,), (1,), sends, own)


def other_kernel(tokens, w_gate, w_up, w_down, *outs):
    left = (tokens.at[0], tokens.at[0], tokens.at[1])
    products(left, (w_gate, w_up, w_down), (0, 0, 1), outs[:3], outs[3])


def term_shapes(count):
    return [shape(count, ROWS, HID)] * 3 + [shape(count, ROWS, HID, dtype=F32)]


def total_kernel(*refs):
    terms, total, out = refs[:-2], refs[-2], refs[-1]
    at = 0
    for i in range(len(terms) // 4):
        own, *others = terms[i * 4 : (i + 1) * 4]
        value = own[...]
        for other in others:
            value += other[...].astype(F32)
        total[at : at + own.shape[0]] = value
        out[at : at + own.shape[0]] = value.astype(BF16)
        at += own.shape[0]


def total_step(terms, later_than=()):
    outs = [shape(3, ROWS, HID, dtype=F32), shape(3, ROWS, HID)]
    return call(total_kernel, terms, outs, 16, later_than)


def grads_kernel(total, other, out, hidden):
    gate, up, hid = (total[i] + other[i].astype(F32) for i in range(3))
    sig = jax.nn.sigmoid(gate)
    silu = gate * sig
    hidden[...] = (silu * up).astype(BF16)
    out[0] = (hid * up * sig * (1.0 + gate * (1.0 - sig))).astype(BF16)
    out[1] = (hid * silu).astype(BF16)


def grads_step(total, half, later_than):
    outs = [shape(2, ROWS, HID), shape(ROWS, HID)]
    return call(grads_kernel, [total, swap_z(half, 4)], outs, 16, later_than)


def swap_all_y(values):
    got = {k: swap_y(values[k - 1], k) for k in (2, 1, 3)}
    return [got[k] for k in (1, 2, 3)]


def backward_kernel(b0, b1, b2, b3, w_gate, w_up, out):
    total = 0.0
    for i, w in enumerate((w_gate, w_up)):
        left = jnp.concatenate([b[i] for b in (b0, b1, b2, b3)], axis=0)
        total += lax.dot_general(
            left, w[...], (((1,), (1,)), ((), ())), preferred_element_type=F32
        )
    for k in range(4):
        out[k] = total[k * ROWS : (k + 1) * ROWS]


def backward(blocks, w_gate, w_up, flops=1):
    outs = [shape(4, ROWS, WIDE, dtype=F32)]
    return call(backward_kernel, [*blocks, w_gate, w_up], outs, 12, flops=flops)[0]


def join_kernel(y_ref, mine, theirs, *outs):
    for j, out in enumerate(outs):
        slot = y_ref[0] ^ j
        out[...] = (mine[slot] + theirs[slot]).astype(out.dtype)


def sum_kernel(own, p1, p2, p3, *outs):
    value = own[...] + p1[...].astype(F32) + p2[...].astype(F32) + p3[...].astype(F32)
    for i, out in enumerate(outs):
        out[...] = value[i * PART : (i + 1) * PART]


def add_kernel(own, p1, p2, p3, out):
    out[...] = (own[...] + p1[...] + p2[...] + p3[...]).astype(BF16)


def reduce_tokens(y, mine, theirs, later_than):
    outs = [shape(ROWS, WIDE, dtype=F32)] + [shape(ROWS, WIDE)] * 3
    total, *parts = call(join_kernel, [mine, theirs], outs, 12, (), y)
    got = [swap_x(part, j + 1) for j, part in enumerate(parts)]
    sums = call(sum_kernel, [total, *got], [shape(PART, WIDE, dtype=F32)] * 4, 8, later_than)
    got = [swap_z(part, j + 1) for j, part in enumerate(sums[1:])]
    return call(add_kernel, [sums[0], *got], [shape(PART, WIDE)], 4)[0]


def rows_kernel(*refs):
    blocks, outs = refs[:8], refs[8:]
    for i, out in enumerate(outs):
        for k, block in enumerate(blocks):
            out[k * ROWS : (k + 1) * ROWS] = block[i]


def hidden_rows_kernel(*refs):
    blocks, out = refs[:4], refs[4]
    for group in range(2):
        for k, block in enumerate(blocks):
            at = (group * 4 + k) * ROWS
            out[at : at + ROWS] = block[group]


def stack_kernel(top, bottom, out):
    out[0] = top[...]
    out[1] = bottom[...]


def dot(left, right):
    return lax.dot_general(
        left, right, (((0,), (0,)), ((), ())), preferred_element_type=F32
    ).astype(BF16)


def gather_tokens(block, later_than=()):
    parts = [block] + [swap_z(block, j) for j in (1, 2, 3)]
    (column,) = call(column_kernel, parts, [shape(ROWS, WIDE)], 4, later_than)
    return [column] + [swap_x(column, j) for j in (1, 2, 3)]


def body(inputs, grad_out, w_gate, w_up, w_down):
    y = (lax.axis_index("tensor") // 2).astype(jnp.int32).reshape(1)
    ready = call(touch_kernel, [w_gate, w_up], [shape(8, 128, dtype=F32)], 8)
    xs = gather_tokens(inputs, ready)
    gs = gather_tokens(grad_out)

    outs = term_shapes(2) + [shape(4, ROWS, WIDE)]
    *sends, own, xs1 = call(gate_up_kernel, [*xs, w_gate, w_up], outs, 20, gs[:1], y)
    terms = [own, *swap_all_y(sends)]
    outs = term_shapes(1) + [shape(2, 4, ROWS, WIDE)]
    *sends, own, tokens1 = call(hid_kernel, [*gs, xs1, w_down], outs, 20, terms[1:], y)
    total1, half1 = total_step([*terms, own, *swap_all_y(sends)])
    tokens2 = swap_core(tokens1)
    args = [tokens2, w_gate, w_up, w_down]
    *sends, own = call(other_kernel, args, term_shapes(3), 20, [own])
    total2, half2 = total_step([own, *swap_all_y(sends)], [half1])

    grads1, hidden1 = grads_step(total1, half1, [half2])
    blocks1 = [grads1] + swap_all_y([grads1] * 3)
    grads2, hidden2 = grads_step(total2, half2, blocks1[1:])
    blocks2 = [grads2] + swap_all_y([grads2] * 3)
    mine = backward(blocks1, w_gate, w_up, 2 * 2 * 4 * ROWS * WIDE * HID)
    theirs = swap_core(backward(blocks2, w_gate, w_up))
    (hidden,) = call(stack_kernel, [hidden1, hidden2], [shape(2, ROWS, HID)], 4, blocks2[1:])
    hiddens = [hidden] + swap_all_y([hidden] * 3)

    rows = [shape(8 * ROWS, HID)]
    gate_grad, up_grad = call(rows_kernel, [*blocks1, *blocks2], rows * 2, 16)
    (hidden,) = call(hidden_rows_kernel, hiddens, rows, 12)
    xs, gs = (
        jnp.concatenate([t[i].reshape(4 * ROWS, WIDE) for t in (tokens1, tokens2)], axis=0)
        for i in range(2)
    )
    grad_gate, grad_up = dot(xs, gate_grad), dot(xs, up_grad)
    before = [grad_gate[:16, :128], grad_up[:16, :128], *hiddens[1:]]
    grad_in = reduce_tokens(y, mine, theirs, before)
    return grad_in, grad_gate, grad_up, dot(hidden, gs)


def solution(mesh):
    return jax.shard_map(
        body,
        mesh=mesh,
        in_specs=(
            P("dp", "tensor"),
            P("dp", "tensor"),
            P("tensor", "dp"),
            P("tensor", "dp"),
            P("dp", "tensor"),
        ),
        out_specs=(P("dp", "tensor"), P("tensor", "dp"), P("tensor", "dp"), P("dp", "tensor")),
        check_vma=False,
    )
```

```python
import functools

import jax
import jax.numpy as jnp
from jax import lax
from jax.experimental import pallas as pl
from jax.experimental.pallas import tpu as pltpu
from jax.sharding import PartitionSpec as P

AXES = ("dp", "tensor")
F32 = jnp.float32
BF16 = jnp.bfloat16
PART = 24
ROWS = 4 * PART
WIDE = 1024
HID = 896
MIB = 1 << 20


def device_index(z, x, core, y):
    return (((z % 4) * 4 + x) * 2 + core) * 8 + y * 2 + z // 4


def swap(value, partner):
    pairs = [
        (device_index(z, x, c, y), device_index(*partner(z, x, c, y)))
        for z in range(8)
        for x in range(4)
        for c in range(2)
        for y in range(4)
    ]
    return lax.ppermute(value, AXES, pairs)


def swap_y(value, mask):
    return swap(value, lambda z, x, c, y: (z, x, c, y ^ mask))


def swap_z(value, mask):
    return swap(value, lambda z, x, c, y: (z ^ mask, x, c, y))


def swap_core(value):
    return swap(value, lambda z, x, c, y: (z, x, c ^ 1, y))


def swap_x(value, mask):
    return swap(value, lambda z, x, c, y: (z, x ^ mask, c, y))


VMEM = pl.BlockSpec(memory_space=pltpu.VMEM)
SMEM = pl.BlockSpec(memory_space=pltpu.SMEM)


def call(kernel, args, outs, vmem, later_than=(), y=None, scratch=(), flops=1):
    scalars = [] if y is None else [y]
    first, last = len(scalars), len(scalars) + len(args)

    def run(*refs):
        kernel(*refs[:last], *refs[last + len(later_than) :])

    return pl.pallas_call(
        run,
        out_shape=outs,
        in_specs=[SMEM] * first + [VMEM] * (len(args) + len(later_than)),
        out_specs=[VMEM] * len(outs),
        scratch_shapes=scratch,
        compiler_params=pltpu.CompilerParams(vmem_limit_bytes=vmem * MIB),
        cost_estimate=pl.CostEstimate(flops=flops, bytes_accessed=1, transcendentals=0),
    )(*scalars, *args, *later_than)


def shape(*dims, dtype=BF16):
    return jax.ShapeDtypeStruct(dims, dtype)


def touch_kernel(w_gate, w_up, out):
    out[...] = w_gate[:8, :128].astype(F32) + w_up[:8, :128].astype(F32)


def column_kernel(*refs):
    for i in range(4):
        refs[4][i * PART : (i + 1) * PART] = refs[i][...]


def products(tokens, weights, dims, sends, own):
    for i, (left, w, dim) in enumerate(zip(tokens, weights, dims)):
        out = lax.dot_general(
            left[...].reshape(4 * ROWS, WIDE),
            w[...],
            (((1,), (dim,)), ((), ())),
            preferred_element_type=F32,
        )
        for k, send in enumerate(sends):
            send[i] = out[(k + 1) * ROWS : (k + 2) * ROWS].astype(BF16)
        own[i] = out[:ROWS]


def gate_up_kernel(y_ref, *refs):
    blocks, weights, sends, own, xs = refs[:4], refs[4:6], refs[6:9], refs[9], refs[10]
    for j, block in enumerate(blocks):
        xs[j ^ y_ref[0]] = block[...]
    products((xs, xs), weights, (0, 0), sends, own)


def hid_kernel(y_ref, *refs):
    blocks, xs, w_down, sends, own, tokens = refs[:4], refs[4], refs[5], refs[6:9], refs[9], refs[10]
    tokens[0] = xs[...]
    for j, block in enumerate(blocks):
        tokens[1, j ^ y_ref[0]] = block[...]
    products((tokens.at[1],), (w_down,), (1,), sends, own)


def other_kernel(tokens, w_gate, w_up, w_down, *outs):
    left = (tokens.at[0], tokens.at[0], tokens.at[1])
    products(left, (w_gate, w_up, w_down), (0, 0, 1), outs[:3], outs[3])


def term_shapes(count):
    return [shape(count, ROWS, HID)] * 3 + [shape(count, ROWS, HID, dtype=F32)]


def total_kernel(*refs):
    terms, total, out = refs[:-2], refs[-2], refs[-1]
    at = 0
    for i in range(len(terms) // 4):
        own, *others = terms[i * 4 : (i + 1) * 4]
        value = own[...]
        for other in others:
            value += other[...].astype(F32)
        total[at : at + own.shape[0]] = value
        out[at : at + own.shape[0]] = value.astype(BF16)
        at += own.shape[0]


def total_step(terms, later_than=()):
    outs = [shape(3, ROWS, HID, dtype=F32), shape(3, ROWS, HID)]
    return call(total_kernel, terms, outs, 16, later_than)


def grads_kernel(total, other, out, hidden):
    gate, up, hid = (total[i] + other[i].astype(F32) for i in range(3))
    sig = jax.nn.sigmoid(gate)
    silu = gate * sig
    hidden[...] = (silu * up).astype(BF16)
    out[0] = (hid * up * sig * (1.0 + gate * (1.0 - sig))).astype(BF16)
    out[1] = (hid * silu).astype(BF16)


def grads_step(total, half, later_than):
    outs = [shape(2, ROWS, HID), shape(ROWS, HID)]
    return call(grads_kernel, [total, swap_z(half, 4)], outs, 16, later_than)


def swap_all_y(values):
    got = {k: swap_y(values[k - 1], k) for k in (2, 1, 3)}
    return [got[k] for k in (1, 2, 3)]


def backward_kernel(b0, b1, b2, b3, w_gate, w_up, out):
    total = 0.0
    for i, w in enumerate((w_gate, w_up)):
        left = jnp.concatenate([b[i] for b in (b0, b1, b2, b3)], axis=0)
        total += lax.dot_general(
            left, w[...], (((1,), (1,)), ((), ())), preferred_element_type=F32
        )
    for k in range(4):
        out[k] = total[k * ROWS : (k + 1) * ROWS]


def backward(blocks, w_gate, w_up, flops=1):
    outs = [shape(4, ROWS, WIDE, dtype=F32)]
    return call(backward_kernel, [*blocks, w_gate, w_up], outs, 12, flops=flops)[0]


def join_kernel(y_ref, mine, theirs, *outs):
    for j, out in enumerate(outs):
        slot = y_ref[0] ^ j
        out[...] = (mine[slot] + theirs[slot]).astype(out.dtype)


def sum_kernel(own, p1, p2, p3, *outs):
    value = own[...] + p1[...].astype(F32) + p2[...].astype(F32) + p3[...].astype(F32)
    for i, out in enumerate(outs):
        out[...] = value[i * PART : (i + 1) * PART]


def add_kernel(own, p1, p2, p3, out):
    out[...] = (own[...] + p1[...] + p2[...] + p3[...]).astype(BF16)


def join_step(y, mine, theirs):
    outs = [shape(ROWS, WIDE, dtype=F32)] + [shape(ROWS, WIDE)] * 3
    return call(join_kernel, [mine, theirs], outs, 12, (), y)


def sum_step(total, parts, later_than):
    got = [swap_x(part, j + 1) for j, part in enumerate(parts)]
    return call(sum_kernel, [total, *got], [shape(PART, WIDE, dtype=F32)] * 4, 8, later_than)


def rows_kernel(index, *refs):
    blocks, out = refs[:8], refs[8]
    for k, block in enumerate(blocks):
        out[k * ROWS : (k + 1) * ROWS] = block[index]


def rows_step(index, blocks, flops=1, later_than=()):
    kernel = functools.partial(rows_kernel, index)
    return call(kernel, blocks, [shape(8 * ROWS, HID)], 16, later_than, flops=flops)[0]


def tokens_kernel(first, second, *outs):
    for i, out in enumerate(outs):
        for k in range(4):
            out[k * ROWS : (k + 1) * ROWS] = first[i, k]
            out[(k + 4) * ROWS : (k + 5) * ROWS] = second[i, k]


def hidden_rows_kernel(*refs):
    blocks, out = refs[:4], refs[4]
    for group in range(2):
        for k, block in enumerate(blocks):
            at = (group * 4 + k) * ROWS
            out[at : at + ROWS] = block[group]


def stack_kernel(top, bottom, out):
    out[0] = top[...]
    out[1] = bottom[...]


def dot(left, right):
    return lax.dot_general(
        left, right, (((0,), (0,)), ((), ())), preferred_element_type=F32
    ).astype(BF16)


def gather_tokens(block, later_than=()):
    parts = [block] + [swap_z(block, j) for j in (1, 2, 3)]
    (column,) = call(column_kernel, parts, [shape(ROWS, WIDE)], 4, later_than)
    return [column] + [swap_x(column, j) for j in (1, 2, 3)]


def body(inputs, grad_out, w_gate, w_up, w_down):
    y = (lax.axis_index("tensor") // 2).astype(jnp.int32).reshape(1)
    ready = call(touch_kernel, [w_gate, w_up], [shape(8, 128, dtype=F32)], 8)
    xs = gather_tokens(inputs, ready)
    gs = gather_tokens(grad_out)

    outs = term_shapes(2) + [shape(4, ROWS, WIDE)]
    *sends, own, xs1 = call(gate_up_kernel, [*xs, w_gate, w_up], outs, 20, gs[:1], y)
    terms = [own, *swap_all_y(sends)]
    outs = term_shapes(1) + [shape(2, 4, ROWS, WIDE)]
    *sends, own, tokens1 = call(hid_kernel, [*gs, xs1, w_down], outs, 20, terms[1:], y)
    total1, half1 = total_step([*terms, own, *swap_all_y(sends)])
    tokens2 = swap_core(tokens1)
    args = [tokens2, w_gate, w_up, w_down]
    *sends, own = call(other_kernel, args, term_shapes(3), 20, [own])
    total2, half2 = total_step([own, *swap_all_y(sends)], [half1])

    grads1, hidden1 = grads_step(total1, half1, [half2])
    blocks1 = [grads1] + swap_all_y([grads1] * 3)
    grads2, hidden2 = grads_step(total2, half2, blocks1[1:])
    blocks2 = [grads2] + swap_all_y([grads2] * 3)
    mine = backward(blocks1, w_gate, w_up, 2 * 2 * 4 * ROWS * WIDE * HID)
    theirs = swap_core(backward(blocks2, w_gate, w_up))
    (hidden,) = call(stack_kernel, [hidden1, hidden2], [shape(2, ROWS, HID)], 4, blocks2[1:])
    hiddens = [hidden] + swap_all_y([hidden] * 3)

    blocks = [*blocks1, *blocks2]
    gate_grad = rows_step(0, blocks, 2 * 8 * ROWS * WIDE * HID)
    total, *parts = join_step(y, mine, theirs)
    outs = [shape(8 * ROWS, WIDE)] * 2
    xs, gs = call(tokens_kernel, [tokens1, tokens2], outs, 16, parts[:1])
    grad_gate = dot(xs, gate_grad)
    sums = sum_step(total, parts, [grad_gate[:16, :128], *hiddens[1:]])
    grad_up = dot(xs, rows_step(1, blocks, 1, sums[:1]))
    (hidden,) = call(hidden_rows_kernel, hiddens, [shape(8 * ROWS, HID)], 12, sums[:1])
    got = [swap_z(part, j + 1) for j, part in enumerate(sums[1:])]
    (grad_in,) = call(add_kernel, [sums[0], *got], [shape(PART, WIDE)], 4)
    return grad_in, grad_gate, grad_up, dot(hidden, gs)


def solution(mesh):
    return jax.shard_map(
        body,
        mesh=mesh,
        in_specs=(
            P("dp", "tensor"),
            P("dp", "tensor"),
            P("tensor", "dp"),
            P("tensor", "dp"),
            P("dp", "tensor"),
        ),
        out_specs=(P("dp", "tensor"), P("tensor", "dp"), P("tensor", "dp"), P("dp", "tensor")),
        check_vma=False,
    )
```

```python
import functools

import jax
import jax.numpy as jnp
from jax import lax
from jax.experimental import pallas as pl
from jax.experimental.pallas import tpu as pltpu
from jax.sharding import PartitionSpec as P

AXES = ("dp", "tensor")
F32 = jnp.float32
BF16 = jnp.bfloat16
PART = 24
ROWS = 4 * PART
WIDE = 1024
HID = 896
MIB = 1 << 20


def device_index(z, x, core, y):
    return (((z % 4) * 4 + x) * 2 + core) * 8 + y * 2 + z // 4


def swap(value, partner):
    pairs = [
        (device_index(z, x, c, y), device_index(*partner(z, x, c, y)))
        for z in range(8)
        for x in range(4)
        for c in range(2)
        for y in range(4)
    ]
    return lax.ppermute(value, AXES, pairs)


def swap_y(value, mask):
    return swap(value, lambda z, x, c, y: (z, x, c, y ^ mask))


def swap_z(value, mask):
    return swap(value, lambda z, x, c, y: (z ^ mask, x, c, y))


def swap_core(value):
    return swap(value, lambda z, x, c, y: (z, x, c ^ 1, y))


def swap_x(value, mask):
    return swap(value, lambda z, x, c, y: (z, x ^ mask, c, y))


VMEM = pl.BlockSpec(memory_space=pltpu.VMEM)
SMEM = pl.BlockSpec(memory_space=pltpu.SMEM)


def call(kernel, args, outs, vmem, later_than=(), y=None, scratch=(), flops=1):
    scalars = [] if y is None else [y]
    first, last = len(scalars), len(scalars) + len(args)

    def run(*refs):
        kernel(*refs[:last], *refs[last + len(later_than) :])

    return pl.pallas_call(
        run,
        out_shape=outs,
        in_specs=[SMEM] * first + [VMEM] * (len(args) + len(later_than)),
        out_specs=[VMEM] * len(outs),
        scratch_shapes=scratch,
        compiler_params=pltpu.CompilerParams(vmem_limit_bytes=vmem * MIB),
        cost_estimate=pl.CostEstimate(flops=flops, bytes_accessed=1, transcendentals=0),
    )(*scalars, *args, *later_than)


def shape(*dims, dtype=BF16):
    return jax.ShapeDtypeStruct(dims, dtype)


def touch_kernel(w_gate, w_up, out):
    out[...] = w_gate[:8, :128].astype(F32) + w_up[:8, :128].astype(F32)


def column_kernel(*refs):
    for i in range(4):
        refs[4][i * PART : (i + 1) * PART] = refs[i][...]


def products(tokens, weights, dims, sends, own):
    for i, (left, w, dim) in enumerate(zip(tokens, weights, dims)):
        out = lax.dot_general(
            left[...].reshape(4 * ROWS, WIDE),
            w[...],
            (((1,), (dim,)), ((), ())),
            preferred_element_type=F32,
        )
        for k, send in enumerate(sends):
            send[i] = out[(k + 1) * ROWS : (k + 2) * ROWS].astype(BF16)
        own[i] = out[:ROWS]


def gate_up_kernel(y_ref, *refs):
    blocks, weights, sends, own, xs = refs[:4], refs[4:6], refs[6:9], refs[9], refs[10]
    for j, block in enumerate(blocks):
        xs[j ^ y_ref[0]] = block[...]
    products((xs, xs), weights, (0, 0), sends, own)


def hid_kernel(y_ref, *refs):
    blocks, xs, w_down, sends, own, tokens = refs[:4], refs[4], refs[5], refs[6:9], refs[9], refs[10]
    tokens[0] = xs[...]
    for j, block in enumerate(blocks):
        tokens[1, j ^ y_ref[0]] = block[...]
    products((tokens.at[1],), (w_down,), (1,), sends, own)


def other_kernel(tokens, w_gate, w_up, w_down, *outs):
    left = (tokens.at[0], tokens.at[0], tokens.at[1])
    products(left, (w_gate, w_up, w_down), (0, 0, 1), outs[:3], outs[3])


def term_shapes(count):
    return [shape(count, ROWS, HID)] * 3 + [shape(count, ROWS, HID, dtype=F32)]


def total_kernel(*refs):
    terms, total, out = refs[:-2], refs[-2], refs[-1]
    at = 0
    for i in range(len(terms) // 4):
        own, *others = terms[i * 4 : (i + 1) * 4]
        value = own[...]
        for other in others:
            value += other[...].astype(F32)
        total[at : at + own.shape[0]] = value
        out[at : at + own.shape[0]] = value.astype(BF16)
        at += own.shape[0]


def total_step(terms, later_than=()):
    outs = [shape(3, ROWS, HID, dtype=F32), shape(3, ROWS, HID)]
    return call(total_kernel, terms, outs, 16, later_than)


def grads_kernel(total, other, out, hidden):
    gate, up, hid = (total[i] + other[i].astype(F32) for i in range(3))
    sig = jax.nn.sigmoid(gate)
    silu = gate * sig
    hidden[...] = (silu * up).astype(BF16)
    out[0] = (hid * up * sig * (1.0 + gate * (1.0 - sig))).astype(BF16)
    out[1] = (hid * silu).astype(BF16)


def grads_step(total, half, later_than):
    outs = [shape(2, ROWS, HID), shape(ROWS, HID)]
    return call(grads_kernel, [total, swap_z(half, 4)], outs, 16, later_than)


def swap_all_y(values):
    got = {k: swap_y(values[k - 1], k) for k in (2, 1, 3)}
    return [got[k] for k in (1, 2, 3)]


def backward_kernel(*refs):
    *blocks, w_gate, w_up, out = refs
    total = 0.0
    for i, w in enumerate((w_gate, w_up)):
        left = jnp.concatenate([b[i] for b in blocks], axis=0)
        total += lax.dot_general(
            left, w[...], (((1,), (1,)), ((), ())), preferred_element_type=F32
        )
    for k in range(len(blocks)):
        out[k] = total[k * ROWS : (k + 1) * ROWS]


def backward(blocks, w_gate, w_up, flops=1, later_than=()):
    outs = [shape(len(blocks), ROWS, WIDE, dtype=F32)]
    return call(backward_kernel, [*blocks, w_gate, w_up], outs, 12, later_than, flops=flops)[0]


def join_kernel(y_ref, mine, low, high, *outs):
    for j, out in enumerate(outs):
        slot = y_ref[0] ^ j

        @pl.when(slot < 2)
        def _():
            out[...] = (mine[slot] + low[slot]).astype(out.dtype)

        @pl.when(slot >= 2)
        def _():
            out[...] = (mine[slot] + high[slot - 2]).astype(out.dtype)


def sum_kernel(own, p1, p2, p3, *outs):
    value = own[...] + p1[...].astype(F32) + p2[...].astype(F32) + p3[...].astype(F32)
    for i, out in enumerate(outs):
        out[...] = value[i * PART : (i + 1) * PART]


def add_kernel(own, p1, p2, p3, out):
    out[...] = (own[...] + p1[...] + p2[...] + p3[...]).astype(BF16)


def join_step(y, mine, theirs):
    outs = [shape(ROWS, WIDE, dtype=F32)] + [shape(ROWS, WIDE)] * 3
    return call(join_kernel, [mine, *theirs], outs, 12, (), y)


def sum_step(total, parts, later_than):
    got = [swap_x(part, j + 1) for j, part in enumerate(parts)]
    return call(sum_kernel, [total, *got], [shape(PART, WIDE, dtype=F32)] * 4, 8, later_than)


def rows_kernel(index, *refs):
    blocks, out = refs[:8], refs[8]
    for k, block in enumerate(blocks):
        out[k * ROWS : (k + 1) * ROWS] = block[index]


def rows_step(index, blocks, flops=1, later_than=()):
    kernel = functools.partial(rows_kernel, index)
    return call(kernel, blocks, [shape(8 * ROWS, HID)], 16, later_than, flops=flops)[0]


def tokens_kernel(first, second, *outs):
    for i, out in enumerate(outs):
        for k in range(4):
            out[k * ROWS : (k + 1) * ROWS] = first[i, k]
            out[(k + 4) * ROWS : (k + 5) * ROWS] = second[i, k]


def hidden_rows_kernel(*refs):
    blocks, out = refs[:4], refs[4]
    for group in range(2):
        for k, block in enumerate(blocks):
            at = (group * 4 + k) * ROWS
            out[at : at + ROWS] = block[group]


def stack_kernel(top, bottom, out):
    out[0] = top[...]
    out[1] = bottom[...]


def dot(left, right):
    return lax.dot_general(
        left, right, (((0,), (0,)), ((), ())), preferred_element_type=F32
    ).astype(BF16)


def gather_tokens(block, later_than=()):
    parts = [block] + [swap_z(block, j) for j in (1, 2, 3)]
    (column,) = call(column_kernel, parts, [shape(ROWS, WIDE)], 4, later_than)
    return [column] + [swap_x(column, j) for j in (1, 2, 3)]


def body(inputs, grad_out, w_gate, w_up, w_down):
    y = (lax.axis_index("tensor") // 2).astype(jnp.int32).reshape(1)
    ready = call(touch_kernel, [w_gate, w_up], [shape(8, 128, dtype=F32)], 8)
    xs = gather_tokens(inputs, ready)
    gs = gather_tokens(grad_out)

    outs = term_shapes(2) + [shape(4, ROWS, WIDE)]
    *sends, own, xs1 = call(gate_up_kernel, [*xs, w_gate, w_up], outs, 20, gs[:1], y)
    terms = [own, *swap_all_y(sends)]
    outs = term_shapes(1) + [shape(2, 4, ROWS, WIDE)]
    *sends, own, tokens1 = call(hid_kernel, [*gs, xs1, w_down], outs, 20, terms[1:], y)
    total1, half1 = total_step([*terms, own, *swap_all_y(sends)])
    tokens2 = swap_core(tokens1)
    args = [tokens2, w_gate, w_up, w_down]
    *sends, own = call(other_kernel, args, term_shapes(3), 20, [own])
    total2, half2 = total_step([own, *swap_all_y(sends)], [half1])

    grads1, hidden1 = grads_step(total1, half1, [half2])
    blocks1 = [grads1] + swap_all_y([grads1] * 3)
    grads2, hidden2 = grads_step(total2, half2, blocks1[1:])
    blocks2 = [grads2] + swap_all_y([grads2] * 3)
    mine = backward(blocks1, w_gate, w_up, 2 * 2 * 4 * ROWS * WIDE * HID)
    low = backward(blocks2[:2], w_gate, w_up)
    high = backward(blocks2[2:], w_gate, w_up, 1, [low])
    theirs = [swap_core(low), swap_core(high)]
    (hidden,) = call(stack_kernel, [hidden1, hidden2], [shape(2, ROWS, HID)], 4, blocks2[1:])
    hiddens = [hidden] + swap_all_y([hidden] * 3)

    blocks = [*blocks1, *blocks2]
    gate_grad = rows_step(0, blocks, 2 * 8 * ROWS * WIDE * HID)
    total, *parts = join_step(y, mine, theirs)
    outs = [shape(8 * ROWS, WIDE)] * 2
    xs, gs = call(tokens_kernel, [tokens1, tokens2], outs, 16, parts[:1])
    grad_gate = dot(xs, gate_grad)
    sums = sum_step(total, parts, [grad_gate[:16, :128], *hiddens[1:3]])
    grad_up = dot(xs, rows_step(1, blocks, 1, sums[:1]))
    (hidden,) = call(hidden_rows_kernel, hiddens, [shape(8 * ROWS, HID)], 12, sums[:1])
    got = [swap_z(part, j + 1) for j, part in enumerate(sums[1:])]
    (grad_in,) = call(add_kernel, [sums[0], *got], [shape(PART, WIDE)], 4)
    return grad_in, grad_gate, grad_up, dot(hidden, gs)


def solution(mesh):
    return jax.shard_map(
        body,
        mesh=mesh,
        in_specs=(
            P("dp", "tensor"),
            P("dp", "tensor"),
            P("tensor", "dp"),
            P("tensor", "dp"),
            P("dp", "tensor"),
        ),
        out_specs=(P("dp", "tensor"), P("tensor", "dp"), P("tensor", "dp"), P("dp", "tensor")),
        check_vma=False,
    )
```
